32 devices in a mesh: row: 4 (over z), col: 8 (over y, x, core).
Axes of the slice: x: 2, y: 2, z: 4, core: 2. Of those that a mesh axis runs over, the one named last changes fastest.
Arguments:
- gradient: float32 [5120, 16384], P('row', 'col'), may hold values from -6 to 6
- eigenbasis: bfloat16 [5120, 5120], P(None, 'row'), may hold values from -0.078125 to 0.078125
- first_moment: float32 [5120, 16384], P('row', 'col'), may hold values from -3 to 3
- second_moment: float32 [5120, 16384], P('row', 'col'), may hold values from 0.05 to 4
Outputs:
- new_first: float32 [5120, 16384], P('row', 'col')
- new_second: float32 [5120, 16384], P('row', 'col')
- direction: float32 [5120, 16384], P('row', 'col')
The draws below stay inside these ranges and needn't reach their ends.
All inputs are finite; a program needn't handle non-finite values.
Results may differ from the reference program's by a relative error of at most 0.003.
Values may be sent and summed in bfloat16 or wider, within the bound.
A program may use at most 192 MiB of HBM per device.

```python
import math
import jax
import jax.numpy as jnp
from jax import lax

M = 5120
COLS = 16384
STEP = 2


def block_scale(own_key, dims, cuts, smallest, top_value):
    def one(axis_at, parts):
        steps = jax.random.uniform(jax.random.fold_in(jax.random.fold_in(own_key, 6), axis_at), (parts,), jnp.float32, smallest / len(cuts), top_value / len(cuts))
        return jnp.repeat(jnp.exp(steps), dims[axis_at] // parts).reshape((-1,) + (1,) * (len(dims) - axis_at - 1))

    loudness = one(*cuts[0])
    for cut in cuts[1:]:
        loudness = loudness * one(*cut)
    return loudness


def bell_draw(own_key, dims, scale, reach, split=(), dtype=jnp.bfloat16):
    values = jax.random.normal(own_key, dims, jnp.float32) * scale
    if len(split) > 0:
        values = block_scale(own_key, dims, split, -0.22, 0.18) * values
    return jnp.clip(values, min=-reach, max=reach).astype(dtype)


def setup_inputs(seed: int = 0) -> dict:
    keys = jax.random.split(jax.random.key(seed), 5)
    gradient = bell_draw(keys[0], (M, COLS), 1.0, 6.0, ((0, 4), (1, 8)), jnp.float32)
    eigenbasis = bell_draw(keys[1], (M, M), M ** -0.5, 0.078125, ((1, 4),))
    first_moment = bell_draw(keys[2], (M, COLS), 0.5, 3.0, ((0, 4), (1, 8)), jnp.float32)
    second_moment = jnp.clip(jnp.exp(math.log(4.0) - 4.3820266 * jax.random.uniform(keys[3], (M, COLS), jnp.float32) ** block_scale(keys[3], (M, COLS), ((0, 4), (1, 8)), -0.2, 0.2)), 0.05, 4.0)
    return {"gradient": gradient, "eigenbasis": eigenbasis, "first_moment": first_moment, "second_moment": second_moment}


def reference(gradient, eigenbasis, first_moment, second_moment):
    grad_low = gradient.astype(jnp.bfloat16)
    rotated = lax.dot_general(eigenbasis, grad_low, (((0,), (0,)), ((), ())), preferred_element_type=jnp.float32)
    new_first = 0.9 * first_moment + 0.1 * rotated
    new_second = 0.99 * second_moment + 0.01 * rotated * rotated
    fix_first = 1.0 - 0.9 ** STEP
    fix_second = 1.0 - 0.99 ** STEP
    step_low = (new_first / fix_first / (jnp.sqrt(new_second / fix_second) + 1e-08)).astype(jnp.bfloat16)
    direction = jnp.dot(eigenbasis, step_low, preferred_element_type=jnp.float32)
    return (new_first, new_second, direction)
```

```python
import jax
import jax.numpy as jnp
from jax import lax
from jax.sharding import PartitionSpec as P

STEP = 2
CHUNKS = 8


def moments(rotated, first_moment, second_moment):
    new_first = 0.9 * first_moment + 0.1 * rotated
    new_second = 0.99 * second_moment + 0.01 * rotated * rotated
    fix_first = 1.0 - 0.9**STEP
    fix_second = 1.0 - 0.99**STEP
    step_low = (new_first / fix_first / (jnp.sqrt(new_second / fix_second) + 1e-08)).astype(
        jnp.bfloat16
    )
    return (new_first, new_second, step_low)


def line_steps(block, terms, n, me):
    whole, total = None, None
    fro, to = [block], [block]
    right, left = 0.0, 0.0
    for s in range(1, n + 1):
        if block is not None and s < n:
            fro.append(lax.ppermute(fro[-1], "row", [(i, i + 1) for i in range(s - 1, n - 1)]))
            to.append(lax.ppermute(to[-1], "row", [(i, i - 1) for i in range(1, n - s + 1)]))
        if terms is not None and s > 1:
            k = s - 1
            ahead = (right + terms[n - k]).astype(jnp.bfloat16)
            behind = (left + terms[k]).astype(jnp.bfloat16)
            if block is not None and k == 1:
                fro[1], to[1], ahead, behind = lax.optimization_barrier((fro[1], to[1], ahead, behind))
            right = lax.ppermute(ahead, "row", [(i, i + 1) for i in range(min(k, n - 1))])
            left = lax.ppermute(behind, "row", [(i, i - 1) for i in range(n - k, n)])
            right, left = right.astype(jnp.float32), left.astype(jnp.float32)
    if block is not None:
        whole = [block] + [jnp.where(me + s < n, to[s], fro[n - s]) for s in range(1, n)]
    if terms is not None:
        total = terms[0] + right + left
    return whole, total


def local(n, gradient, eigenbasis, first_moment, second_moment):
    me = lax.axis_index("row")
    rows, cols = gradient.shape
    chunks = CHUNKS if cols % (CHUNKS * 256) == 0 else 1
    w = cols // chunks
    rolled = jnp.concatenate([eigenbasis, eigenbasis], 0)
    rolled = lax.dynamic_slice_in_dim(rolled, me * rows, n * rows, 0)
    first = second = direction = jnp.zeros((rows, cols), jnp.float32)
    whole, terms = None, None
    for p in range(chunks + 2):
        block = None
        if p < chunks:
            block = gradient[:, p * w : (p + 1) * w]
        block, whole, terms = lax.optimization_barrier((block, whole, terms))
        if block is not None:
            block = block.astype(jnp.bfloat16)
        next_whole, total = line_steps(block, terms, n, me)
        terms = None
        if whole is not None:
            c = (p - 1) * w
            rotated = lax.dot_general(
                rolled, jnp.concatenate(whole, 0), (((0,), (0,)), ((), ())), preferred_element_type=jnp.float32
            )
            new_first, new_second, step_low = moments(
                rotated, first_moment[:, c : c + w], second_moment[:, c : c + w]
            )
            terms = jnp.dot(rolled, step_low, preferred_element_type=jnp.float32)
            terms = [terms[k * rows : (k + 1) * rows] for k in range(n)]
            first = lax.dynamic_update_slice(first, new_first, (0, c))
            second = lax.dynamic_update_slice(second, new_second, (0, c))
        if total is not None:
            direction = lax.dynamic_update_slice(direction, total, (0, (p - 2) * w))
        whole = next_whole
    return first, second, direction


def solution(mesh):
    n = mesh.shape["row"]
    in_specs = (P("row", "col"), P(None, "row"), P("row", "col"), P("row", "col"))
    out_specs = (P("row", "col"), P("row", "col"), P("row", "col"))
    return jax.shard_map(
        lambda *a: local(n, *a), mesh=mesh, in_specs=in_specs, out_specs=out_specs, check_vma=False
    )
```

```python
import jax
import jax.numpy as jnp
from jax import lax
from jax.sharding import PartitionSpec as P

STEP = 2
CHUNKS = 8


def moments(rotated, first_moment, second_moment):
    new_first = 0.9 * first_moment + 0.1 * rotated
    new_second = 0.99 * second_moment + 0.01 * rotated * rotated
    fix_first = 1.0 - 0.9**STEP
    fix_second = 1.0 - 0.99**STEP
    step_low = (new_first / fix_first / (jnp.sqrt(new_second / fix_second) + 1e-08)).astype(
        jnp.bfloat16
    )
    return (new_first, new_second, step_low)


def line_steps(block, terms, n, me):
    whole, total = None, None
    fro, to = [block], [block]
    right, left = 0.0, 0.0
    for s in range(1, n + 1):
        if block is not None and s < n:
            fro.append(lax.ppermute(fro[-1], "row", [(i, i + 1) for i in range(s - 1, n - 1)]))
            to.append(lax.ppermute(to[-1], "row", [(i, i - 1) for i in range(1, n - s + 1)]))
        if terms is not None and s > 1:
            k = s - 1
            ahead = (right + terms[n - k]).astype(jnp.bfloat16)
            behind = (left + terms[k]).astype(jnp.bfloat16)
            right = lax.ppermute(ahead, "row", [(i, i + 1) for i in range(min(k, n - 1))])
            left = lax.ppermute(behind, "row", [(i, i - 1) for i in range(n - k, n)])
            right, left = right.astype(jnp.float32), left.astype(jnp.float32)
    if block is not None:
        whole = [block] + [jnp.where(me + s < n, to[s], fro[n - s]) for s in range(1, n)]
    if terms is not None:
        total = terms[0] + right + left
    return whole, total


def local(n, gradient, eigenbasis, first_moment, second_moment):
    me = lax.axis_index("row")
    rows, cols = gradient.shape
    chunks = CHUNKS if cols % (CHUNKS * 256) == 0 else 1
    w = cols // chunks
    first = second = direction = jnp.zeros((rows, cols), jnp.float32)
    older, whole, terms = None, None, None
    for p in range(chunks + 2):
        block = None
        if p < chunks:
            block = gradient[:, p * w : (p + 1) * w]
        if older is not None and block is not None:
            block, older, terms = lax.optimization_barrier((block, older, terms))
        if p == 1:
            eigenbasis, whole = lax.optimization_barrier((eigenbasis, whole))
            rolled = lax.dynamic_slice_in_dim(
                jnp.concatenate([eigenbasis, eigenbasis], 0), me * rows, n * rows, 0
            )
        if block is not None:
            block = block.astype(jnp.bfloat16)
        next_whole, total = line_steps(block, terms, n, me)
        terms = None
        if whole is not None:
            c = (p - 1) * w
            rotated = lax.dot_general(
                rolled, jnp.concatenate(whole, 0), (((0,), (0,)), ((), ())), preferred_element_type=jnp.float32
            )
            new_first, new_second, step_low = moments(
                rotated, first_moment[:, c : c + w], second_moment[:, c : c + w]
            )
            terms = jnp.dot(rolled, step_low, preferred_element_type=jnp.float32)
            terms = [terms[k * rows : (k + 1) * rows] for k in range(n)]
            first = lax.dynamic_update_slice(first, new_first, (0, c))
            second = lax.dynamic_update_slice(second, new_second, (0, c))
        if total is not None:
            direction = lax.dynamic_update_slice(direction, total, (0, (p - 2) * w))
        older, whole = whole, next_whole
    return first, second, direction


def solution(mesh):
    n = mesh.shape["row"]
    in_specs = (P("row", "col"), P(None, "row"), P("row", "col"), P("row", "col"))
    out_specs = (P("row", "col"), P("row", "col"), P("row", "col"))
    return jax.shard_map(
        lambda *a: local(n, *a), mesh=mesh, in_specs=in_specs, out_specs=out_specs, check_vma=False
    )
```

```python
import jax
import jax.numpy as jnp
from jax import lax
from jax.sharding import PartitionSpec as P

STEP = 2
CHUNKS = 8


def moments(rotated, first_moment, second_moment):
    new_first = 0.9 * first_moment + 0.1 * rotated
    new_second = 0.99 * second_moment + 0.01 * rotated * rotated
    fix_first = 1.0 - 0.9**STEP
    fix_second = 1.0 - 0.99**STEP
    step_low = (new_first / fix_first / (jnp.sqrt(new_second / fix_second) + 1e-08)).astype(
        jnp.bfloat16
    )
    return (new_first, new_second, step_low)


def line_steps(block, terms, upcoming, prior, n, me):
    whole = None
    fro, to = [block], [block]
    right, left = 0.0, 0.0
    for s in range(1, n + 1):
        ahead, behind = None, None
        if terms is not None and s > 1:
            ahead = (right + terms[n - s + 1]).astype(jnp.bfloat16)
            behind = (left + terms[s - 1]).astype(jnp.bfloat16)
        if s == 2:
            fro[-1], to[-1], ahead, behind, prior = lax.optimization_barrier((fro[-1], to[-1], ahead, behind, prior))
        elif s == n and block is not None:
            fro[-1], to[-1], ahead, behind, upcoming = lax.optimization_barrier(
                (fro[-1], to[-1], ahead, behind, upcoming)
            )
        elif s > 2:
            fro[-1], to[-1], ahead, behind = lax.optimization_barrier((fro[-1], to[-1], ahead, behind))
        if block is not None and s < n:
            fro.append(lax.ppermute(fro[-1], "row", [(i, i + 1) for i in range(s - 1, n - 1)]))
            to.append(lax.ppermute(to[-1], "row", [(i, i - 1) for i in range(1, n - s + 1)]))
        if ahead is not None:
            k = s - 1
            right = lax.ppermute(ahead, "row", [(i, i + 1) for i in range(k)])
            left = lax.ppermute(behind, "row", [(i, i - 1) for i in range(n - k, n)])
    if block is not None:
        whole = [block] + [jnp.where(me + s < n, to[s], fro[n - s]) for s in range(1, n)]
    arrived = None if terms is None else (right, left)
    return whole, arrived, upcoming, prior


def local(n, gradient, eigenbasis, first_moment, second_moment):
    me = lax.axis_index("row")
    rows, cols = gradient.shape
    chunks = CHUNKS if cols % (CHUNKS * 256) == 0 else 1
    w = cols // chunks
    rolled = jnp.concatenate([eigenbasis, eigenbasis], 0)
    rolled = lax.dynamic_slice_in_dim(rolled, me * rows, n * rows, 0)
    first, second, direction = (jnp.full((rows, cols), v, jnp.float32) for v in (0.0, 1.0, 2.0))
    whole, prior, own = None, None, None
    blocks = [gradient[:, c * w : (c + 1) * w].astype(jnp.bfloat16) for c in range(chunks)] + [None]
    block = blocks[0]
    for p in range(chunks + 1):
        terms = None
        if whole is not None:
            c = (p - 1) * w
            rotated = lax.dot_general(
                rolled, jnp.concatenate(whole, 0), (((0,), (0,)), ((), ())), preferred_element_type=jnp.float32
            )
            new_first, new_second, step_low = moments(
                rotated, first_moment[:, c : c + w], second_moment[:, c : c + w]
            )
            terms = jnp.dot(rolled, step_low, preferred_element_type=jnp.float32)
            terms = [terms[k * rows : (k + 1) * rows] for k in range(n)]
            first = lax.dynamic_update_slice(first, new_first, (0, c))
            second = lax.dynamic_update_slice(second, new_second, (0, c))
        upcoming = blocks[p + 1] if p < chunks else None
        whole, arrived, block, prior = line_steps(block, terms, upcoming, prior, n, me)
        if prior is not None:
            direction = lax.dynamic_update_slice(direction, own + prior[0] + prior[1], (0, (p - 2) * w))
        prior, own = arrived, None if terms is None else terms[0]
    direction = lax.dynamic_update_slice(direction, own + prior[0] + prior[1], (0, (chunks - 1) * w))
    return first, second, direction


def solution(mesh):
    n = mesh.shape["row"]
    in_specs = (P("row", "col"), P(None, "row"), P("row", "col"), P("row", "col"))
    out_specs = (P("row", "col"), P("row", "col"), P("row", "col"))
    return jax.shard_map(
        lambda *a: local(n, *a), mesh=mesh, in_specs=in_specs, out_specs=out_specs, check_vma=False
    )
```
